512 devices in a mesh: row: 16 (over z), col: 8 (over x, core), rep: 4 (over y).
Axes of the slice: x: 4, y: 4, z: 16, core: 2. Of those that a mesh axis runs over, the one named last changes fastest.
Arguments:
- density: bfloat16 [6144, 6144], P('row', 'col'), as said below
- keep_square: int32 [48, 48], P('row', 'col'), may hold values 0 or 1
- keep_cube: int32 [48, 48], P('row', 'col'), may hold values 0 or 1
Outputs:
- purified: float32 [6144, 6144], P(('row', 'rep'), 'col')
The draws below stay inside these ranges and needn't reach their ends.
Inputs may be any that keep to these rules, and one draw needn't show every extreme that they name: density is symmetric; its 128 x 128 diagonal blocks are always occupied, any other block may be zero or occupied at any distance from the diagonal.
All inputs are finite; a program needn't handle non-finite values. No bound on the sum of `keep_square` or of `keep_cube` on one device may be relied on, other than what follows from the above.
Results may differ from the reference program's by a relative error of at most 0.002.
Values may be sent and summed in bfloat16 or wider, within the bound.
No kernel may reach another device: no remote copies, remote signals or barrier semaphores. Data moves between devices by JAX's collectives and lax.ppermute only.
A program may use at most 64 MiB of HBM per device.

```python
import jax
import jax.numpy as jnp

BLK = 128
MAT = 6144
NBLK = 48


def draw_density(key, part):
    block_count = MAT // BLK
    key_bits, key_values = jax.random.split(jax.random.fold_in(key, 17), 2)
    raw_bits = jax.random.randint(key_bits, (block_count, block_count), 0, 4)
    upper = jnp.triu((raw_bits == 0).astype(jnp.int32), 1)
    pattern = upper + upper.T + jnp.eye(block_count, dtype=jnp.int32) > 0
    blocks = jnp.broadcast_to(pattern.astype(jnp.float32)[:, None, :, None], (block_count, BLK, block_count, BLK)).reshape(MAT, MAT)
    values = jax.random.normal(key_values, (MAT, MAT), jnp.float32)
    values = (values + values.T) * 0.7071
    return (values * blocks * ((block_count // 4 + 1) * BLK * 1.0) ** (-0.25)).astype(jnp.bfloat16)


def plant(result, key, low, top_value):
    index_at = [jax.random.randint(jax.random.fold_in(key, axis), (), 0, length) for axis, length in enumerate(result.shape)]
    widest = result.shape.index(max(result.shape))
    next_to = index_at[:widest] + [(index_at[widest] + 1) % result.shape[widest]] + index_at[widest + 1:]
    return result.at[tuple(index_at)].set(low).at[tuple(next_to)].set(top_value)


def setup_inputs(seed: int = 0) -> dict:
    keys = jax.random.split(jax.random.key(seed), 4)
    density = draw_density(jax.random.fold_in(keys[3], 71), 0)
    keep_square = plant((jax.random.randint(keys[1], (NBLK, NBLK), 0, 4) < 3).astype(jnp.int32), jax.random.fold_in(keys[1], 1), 0, 1)
    keep_cube = plant((jax.random.randint(keys[2], (NBLK, NBLK), 0, 4) < 3).astype(jnp.int32), jax.random.fold_in(keys[2], 1), 0, 1)
    return dict(density=density, keep_square=keep_square, keep_cube=keep_cube)


def widen(mask):
    count = mask.shape[0]
    blocks = jnp.broadcast_to(mask.astype(jnp.float32)[:, None, :, None], (count, BLK, count, BLK))
    return blocks.reshape(count * BLK, count * BLK)


def reference(density, keep_square, keep_cube):
    square = jnp.dot(density, density, preferred_element_type=jnp.float32) * widen(keep_square)
    square_low = square.astype(jnp.bfloat16)
    cube = jnp.dot(square_low, density, preferred_element_type=jnp.float32) * widen(keep_cube)
    return 3.0 * square - 2.0 * cube
```

```python
import jax
import jax.numpy as jnp
from jax import lax
from jax.sharding import PartitionSpec as P

BLK = 128
TOP = 16384.0
TINY = 1.1754943508222875e-38
PAD = 16


def encode(piece):
    values = piece.astype(jnp.float32)
    largest = jnp.max(jnp.abs(values), axis=0, keepdims=True)
    exponent = jnp.floor(jnp.log2(jnp.maximum(largest, TINY)))
    coded = (values * jnp.exp2(-exponent) * TOP).astype(jnp.float16)
    header = jnp.broadcast_to(exponent, (PAD, piece.shape[1])).astype(jnp.float16)
    return jnp.concatenate([coded, header], axis=0)


def decode(coded, count):
    parts = coded.reshape(count, -1, coded.shape[1]).astype(jnp.float32)
    height = parts.shape[1] - PAD
    scale = jnp.exp2(parts[:, height : height + 1, :])
    values = (parts[:, :height, :] * (1.0 / TOP) * scale).astype(jnp.bfloat16)
    return values.reshape(count * height, coded.shape[1])


def local(density, keep_square, keep_cube):
    tile_rows, tile_cols = density.shape
    reps = lax.axis_size("rep")
    row_count = lax.axis_size("row")
    col_count = lax.axis_size("col")
    rep = lax.axis_index("rep")
    own = tile_rows // reps
    halves = tile_cols // tile_rows

    def section(array):
        cut = [
            lax.dynamic_slice_in_dim(array, half * tile_rows + rep * own, own, 0)
            for half in range(halves)
        ]
        return jnp.concatenate(cut, axis=0)

    right_piece = lax.dynamic_slice_in_dim(density, rep * own, own, 0)
    left_piece = section(density.T)
    left = decode(lax.all_gather(encode(left_piece), "col", axis=0, tiled=True), col_count)
    right = decode(lax.all_gather(encode(right_piece), "row", axis=0, tiled=True), row_count)

    def contract(a, b):
        return lax.dot_general(a, b, (((0,), (0,)), ((), ())), preferred_element_type=jnp.float32)

    partial = contract(right, left)
    partial = partial.reshape(halves, reps, own, tile_rows).transpose(1, 0, 2, 3)
    partial = partial.reshape(reps, halves * own, tile_rows)
    square_t = jnp.sum(lax.all_to_all(partial, "rep", 0, 0), axis=0)
    mask_rows = section(jnp.repeat(keep_square.T.astype(jnp.float32), BLK, axis=0))
    square_t = square_t * jnp.repeat(mask_rows, BLK, axis=1)

    low = decode(
        lax.all_gather(encode(square_t.astype(jnp.bfloat16)), "col", axis=0, tiled=True), col_count
    )
    cube = contract(low, right)
    mask = jnp.repeat(jnp.repeat(keep_cube.astype(jnp.float32), BLK, axis=0), BLK, axis=1)
    placed = jnp.zeros((tile_cols, tile_rows), jnp.float32)
    for half in range(halves):
        placed = lax.dynamic_update_slice_in_dim(
            placed, square_t[half * own : (half + 1) * own], half * tile_rows + rep * own, 0
        )
    total = 3.0 * placed.T - 2.0 * cube * mask
    pieces = lax.all_to_all(total.reshape(reps, own, tile_cols), "rep", 0, 0)
    return jnp.sum(pieces, axis=0)


def solution(mesh):
    return jax.shard_map(
        local,
        mesh=mesh,
        in_specs=(P("row", "col"), P("row", "col"), P("row", "col")),
        out_specs=P(("row", "rep"), "col"),
        check_vma=False,
    )
```

```python
import functools

import jax
import jax.numpy as jnp
from jax import lax
from jax.experimental import pallas as pl
from jax.experimental.pallas import tpu as pltpu
from jax.sharding import PartitionSpec as P

BLK = 128
TOP = 8192.0
LOWEST, HIGHEST = -100.0, 126.0
HEAD = 8

SMEM = pl.BlockSpec(memory_space=pltpu.SMEM)
VMEM = pl.BlockSpec(memory_space=pltpu.VMEM)


def call(kernel, out_shape, in_specs, scratch=()):
    return pl.pallas_call(
        kernel,
        out_shape=out_shape,
        in_specs=in_specs,
        scratch_shapes=list(scratch),
        compiler_params=pltpu.CompilerParams(vmem_limit_bytes=48 << 20),
    )


def contract(a, b):
    return lax.dot_general(a, b, (((0,), (0,)), ((), ())), preferred_element_type=jnp.float32)


def scaled(values):
    largest = jnp.max(jnp.abs(values), axis=0, keepdims=True)
    exponent = jnp.floor(jnp.log2(jnp.maximum(largest, 2.0**LOWEST)))
    exponent = jnp.clip(exponent, LOWEST, HIGHEST)
    return values * jnp.exp2(-exponent) * TOP, exponent


def store_coded(ref, values):
    coded, exponent = scaled(values)
    height = values.shape[0]
    ref[:height, :] = coded.astype(jnp.bfloat16)
    ref[height:, :] = jnp.broadcast_to(exponent, (ref.shape[0] - height, values.shape[1])).astype(
        jnp.bfloat16
    )


def gather(coded, axis):
    whole = lax.all_gather(coded.astype(jnp.float16), axis)
    count, height, width = whole.shape
    height -= HEAD
    scale = jnp.exp2(whole[:, height : height + 1, :].astype(jnp.float32))
    values = whole[:, :height, :].astype(jnp.float32) * (1.0 / TOP) * scale
    return values.astype(jnp.bfloat16).reshape(count * height, width)


def prepare(own, halves, rep_ref, tile_ref, right_ref, left_ref, turned):
    rows = tile_ref.shape[0]
    start = pl.multiple_of(rep_ref[0] * own, own)
    store_coded(right_ref, tile_ref[pl.ds(start, own), :].astype(jnp.float32))
    turned[...] = tile_ref[...].T
    for half in range(halves):
        piece = turned[pl.ds(pl.multiple_of(half * rows + start, own), own), :]
        for to in range(left_ref.shape[0]):
            left_ref[to, half * own : (half + 1) * own, :] = piece


def square_part(own, halves, right_ref, left_ref, out_ref):
    product = contract(right_ref[...], left_ref[...])
    rows = product.shape[0] // halves
    for rep in range(out_ref.shape[0]):
        for half in range(halves):
            first = half * rows + rep * own
            out_ref[rep, half * own : (half + 1) * own, :] = product[first : first + own, :]


def square_sum(own, halves, rep_ref, keep_ref, parts_ref, square_ref, low_ref):
    total = parts_ref[0]
    for rep in range(1, parts_ref.shape[0]):
        total = total + parts_ref[rep]
    rows = parts_ref.shape[2]
    per_half = rows // BLK
    start = rep_ref[0] * own
    for half in range(halves):
        block = lax.div(lax.broadcasted_iota(jnp.int32, (own, BLK), 0) + start, BLK)
        for across in range(rows // BLK):
            kept = jnp.zeros((own, BLK), jnp.float32)
            for down in range(per_half):
                keep = keep_ref[across, half * per_half + down].astype(jnp.float32)
                kept = jnp.where(block == down, keep, kept)
            at = slice(half * own, (half + 1) * own), slice(across * BLK, (across + 1) * BLK)
            square_ref[at] = total[at] * kept
    store_coded(low_ref, square_ref[...].astype(jnp.bfloat16).astype(jnp.float32))


def cube_part(own, halves, rep_ref, keep_ref, low_ref, right_ref, square_ref, out_ref, placed):
    rows = out_ref.shape[0]
    start = pl.multiple_of(rep_ref[0] * own, own)
    placed[...] = jnp.zeros_like(placed)
    for half in range(halves):
        placed[pl.ds(pl.multiple_of(half * rows + start, own), own), :] = (
            3.0 * square_ref[half * own : (half + 1) * own, :]
        )
    product = contract(low_ref[...], right_ref[...])
    for down in range(rows // BLK):
        for across in range(out_ref.shape[1] // BLK):
            at = slice(down * BLK, (down + 1) * BLK), slice(across * BLK, (across + 1) * BLK)
            factor = -2.0 * keep_ref[down, across].astype(jnp.float32)
            out_ref[at] = placed[at[1], at[0]].T + factor * product[at]


def local(density, keep_square, keep_cube):
    rows, cols = density.shape
    reps, col_count = lax.axis_size("rep"), lax.axis_size("col")
    own, halves = rows // reps, cols // rows
    rep = lax.axis_index("rep").astype(jnp.int32).reshape(1)
    shape = jax.ShapeDtypeStruct
    part = halves * own

    right_coded, left_copies = call(
        functools.partial(prepare, own, halves),
        (shape((own + HEAD, cols), jnp.bfloat16), shape((col_count, part, rows), jnp.bfloat16)),
        [SMEM, VMEM],
        [pltpu.VMEM((cols, rows), jnp.bfloat16)],
    )(rep, density)
    left = lax.all_to_all(left_copies, "col", 0, 0).reshape(col_count * part, rows)
    right = gather(right_coded, "row")
    parts = call(
        functools.partial(square_part, own, halves),
        shape((reps, part, rows), jnp.float32),
        [VMEM, VMEM],
    )(right, left)
    parts = lax.all_to_all(parts, "rep", 0, 0)
    square, low_coded = call(
        functools.partial(square_sum, own, halves),
        (shape((part, rows), jnp.float32), shape((part + HEAD, rows), jnp.bfloat16)),
        [SMEM, SMEM, VMEM],
    )(rep, keep_square, parts)
    low = gather(low_coded, "col")
    total = call(
        functools.partial(cube_part, own, halves),
        shape((rows, cols), jnp.float32),
        [SMEM, SMEM, VMEM, VMEM, VMEM],
        [pltpu.VMEM((cols, rows), jnp.float32)],
    )(rep, keep_cube, low, right, square)
    pieces = lax.all_to_all(total.reshape(reps, own, cols), "rep", 0, 0)
    return jnp.sum(pieces, axis=0)


def solution(mesh):
    return jax.shard_map(
        local,
        mesh=mesh,
        in_specs=(P("row", "col"), P("row", "col"), P("row", "col")),
        out_specs=P(("row", "rep"), "col"),
        check_vma=False,
    )
```

```python
import functools

import jax
import jax.numpy as jnp
from jax import lax
from jax.experimental import pallas as pl
from jax.experimental.pallas import tpu as pltpu
from jax.sharding import PartitionSpec as P

BLK = 128
TOP = 8192.0
LOWEST, HIGHEST = -100.0, 126.0
HEAD = 8

SMEM = pl.BlockSpec(memory_space=pltpu.SMEM)
VMEM = pl.BlockSpec(memory_space=pltpu.VMEM)


def call(kernel, out_shape, in_specs, scratch=()):
    return pl.pallas_call(
        kernel,
        out_shape=out_shape,
        in_specs=in_specs,
        scratch_shapes=list(scratch),
        compiler_params=pltpu.CompilerParams(vmem_limit_bytes=48 << 20),
    )


def contract(a, b):
    return lax.dot_general(a, b, (((0,), (0,)), ((), ())), preferred_element_type=jnp.float32)


def scaled(values):
    largest = jnp.max(jnp.abs(values), axis=0, keepdims=True)
    exponent = jnp.floor(jnp.log2(jnp.maximum(largest, 2.0**LOWEST)))
    exponent = jnp.clip(exponent, LOWEST, HIGHEST)
    return values * jnp.exp2(-exponent) * TOP, exponent


def store_coded(ref, values):
    coded, exponent = scaled(values)
    height = values.shape[0]
    ref[:height, :] = coded.astype(ref.dtype)
    ref[height:, :] = jnp.broadcast_to(exponent, (HEAD, values.shape[1])).astype(ref.dtype)


def decode(pieces):
    height = pieces.shape[1] - HEAD
    scale = jnp.exp2(pieces[:, height : height + 1, :].astype(jnp.float32))
    return pieces[:, :height, :].astype(jnp.float32) * (1.0 / TOP) * scale


def gather(coded, axis):
    values = decode(lax.all_gather(coded.astype(jnp.float16), axis)).astype(jnp.bfloat16)
    return values.reshape(-1, values.shape[2])


def prepare(own, halves, rep_ref, tile_ref, right_ref, left_ref, turned):
    rows = tile_ref.shape[0]
    start = pl.multiple_of(rep_ref[0] * own, own)
    store_coded(right_ref, tile_ref[pl.ds(start, own), :].astype(jnp.float32))
    turned[...] = tile_ref[...].T
    for half in range(halves):
        piece = turned[pl.ds(pl.multiple_of(half * rows + start, own), own), :]
        for to in range(left_ref.shape[0]):
            left_ref[to, half * own : (half + 1) * own, :] = piece


def square_part(own, halves, right_ref, left_ref, out_ref):
    product = contract(right_ref[...], left_ref[...])
    rows = product.shape[0] // halves
    for rep in range(out_ref.shape[0]):
        for half in range(halves):
            first = half * rows + rep * own
            out_ref[rep, half * own : (half + 1) * own, :] = product[first : first + own, :]


def square_sum(own, halves, rep_ref, keep_ref, parts_ref, square_ref, low_ref):
    total = parts_ref[0]
    for rep in range(1, parts_ref.shape[0]):
        total = total + parts_ref[rep]
    rows = parts_ref.shape[2]
    per_half = rows // BLK
    start = rep_ref[0] * own
    for half in range(halves):
        block = lax.div(lax.broadcasted_iota(jnp.int32, (own, BLK), 0) + start, BLK)
        for across in range(rows // BLK):
            kept = jnp.zeros((own, BLK), jnp.float32)
            for down in range(per_half):
                keep = keep_ref[across, half * per_half + down].astype(jnp.float32)
                kept = jnp.where(block == down, keep, kept)
            at = slice(half * own, (half + 1) * own), slice(across * BLK, (across + 1) * BLK)
            square_ref[at] = total[at] * kept
    store_coded(low_ref, square_ref[...].astype(jnp.bfloat16).astype(jnp.float32))


def cube_part(own, halves, rep_ref, keep_ref, low_ref, right_ref, square_ref, out_ref, placed, total):
    rows, cols = total.shape
    start = pl.multiple_of(rep_ref[0] * own, own)
    placed[...] = jnp.zeros_like(placed)
    for half in range(halves):
        placed[pl.ds(pl.multiple_of(half * rows + start, own), own), :] = (
            3.0 * square_ref[half * own : (half + 1) * own, :]
        )
    product = contract(low_ref[...], right_ref[...])
    for down in range(rows // BLK):
        for across in range(cols // BLK):
            at = slice(down * BLK, (down + 1) * BLK), slice(across * BLK, (across + 1) * BLK)
            factor = -2.0 * keep_ref[down, across].astype(jnp.float32)
            total[at] = placed[at[1], at[0]].T + factor * product[at]
    for rep in range(out_ref.shape[0]):
        store_coded(out_ref.at[rep], total[rep * own : (rep + 1) * own, :])


def local(density, keep_square, keep_cube):
    rows, cols = density.shape
    reps, col_count = lax.axis_size("rep"), lax.axis_size("col")
    own, halves = rows // reps, cols // rows
    rep = lax.axis_index("rep").astype(jnp.int32).reshape(1)
    shape = jax.ShapeDtypeStruct
    part = halves * own

    right_coded, left_copies = call(
        functools.partial(prepare, own, halves),
        (shape((own + HEAD, cols), jnp.bfloat16), shape((col_count, part, rows), jnp.bfloat16)),
        [SMEM, VMEM],
        [pltpu.VMEM((cols, rows), jnp.bfloat16)],
    )(rep, density)
    left = lax.all_to_all(left_copies, "col", 0, 0).reshape(col_count * part, rows)
    right = gather(right_coded, "row")
    parts = call(
        functools.partial(square_part, own, halves),
        shape((reps, part, rows), jnp.float32),
        [VMEM, VMEM],
    )(right, left)
    parts = lax.all_to_all(parts, "rep", 0, 0)
    square, low_coded = call(
        functools.partial(square_sum, own, halves),
        (shape((part, rows), jnp.float32), shape((part + HEAD, rows), jnp.bfloat16)),
        [SMEM, SMEM, VMEM],
    )(rep, keep_square, parts)
    low = gather(low_coded, "col")
    total = call(
        functools.partial(cube_part, own, halves),
        shape((reps, own + HEAD, cols), jnp.float32),
        [SMEM, SMEM, VMEM, VMEM, VMEM],
        [pltpu.VMEM((cols, rows), jnp.float32), pltpu.VMEM((rows, cols), jnp.float32)],
    )(rep, keep_cube, low, right, square)
    return jnp.sum(decode(lax.all_to_all(total.astype(jnp.float16), "rep", 0, 0)), axis=0)


def solution(mesh):
    return jax.shard_map(
        local,
        mesh=mesh,
        in_specs=(P("row", "col"), P("row", "col"), P("row", "col")),
        out_specs=P(("row", "rep"), "col"),
        check_vma=False,
    )
```

```python
import functools

import jax
import jax.numpy as jnp
from jax import lax
from jax.experimental import pallas as pl
from jax.experimental.pallas import tpu as pltpu
from jax.sharding import PartitionSpec as P

BLK = 128
TOP = 8192.0
LOWEST, HIGHEST = -100.0, 126.0
HEAD = 8

SMEM = pl.BlockSpec(memory_space=pltpu.SMEM)
VMEM = pl.BlockSpec(memory_space=pltpu.VMEM)


def call(kernel, out_shape, in_specs, scratch=()):
    return pl.pallas_call(
        kernel,
        out_shape=out_shape,
        in_specs=in_specs,
        scratch_shapes=list(scratch),
        compiler_params=pltpu.CompilerParams(vmem_limit_bytes=32 << 20),
    )


def contract(a, b):
    return lax.dot_general(a, b, (((0,), (0,)), ((), ())), preferred_element_type=jnp.float32)


def scaled(values):
    largest = jnp.max(jnp.abs(values), axis=0, keepdims=True)
    exponent = jnp.floor(jnp.log2(jnp.maximum(largest, 2.0**LOWEST)))
    exponent = jnp.clip(exponent, LOWEST, HIGHEST)
    return values * jnp.exp2(-exponent) * TOP, exponent


def store_coded(ref, values):
    coded, exponent = scaled(values)
    height = values.shape[0]
    ref[:height, :] = coded.astype(ref.dtype)
    ref[height:, :] = jnp.broadcast_to(exponent, (HEAD, values.shape[1])).astype(ref.dtype)


def store_packed(ref, values):
    coded, exponent = scaled(values)
    height, width = values.shape
    groups = width // BLK
    for group in range(groups):
        columns = slice(group * BLK, (group + 1) * BLK)
        ref[group * height : (group + 1) * height, :] = coded[:, columns].astype(ref.dtype)
    rows = [exponent[:, group * BLK : (group + 1) * BLK] for group in range(groups)]
    rows.append(jnp.zeros((HEAD - groups, BLK), jnp.float32))
    ref[groups * height :, :] = jnp.concatenate(rows, axis=0).astype(ref.dtype)


def decode(pieces):
    height = pieces.shape[1] - HEAD
    scale = jnp.exp2(pieces[:, height : height + 1, :].astype(jnp.float32))
    return pieces[:, :height, :].astype(jnp.float32) * (1.0 / TOP) * scale


def gather(packed, axis):
    return lax.all_gather(packed.astype(jnp.float16), axis).astype(jnp.bfloat16)


def panel(ref, groups):
    count, height, _ = ref.shape
    height = (height - HEAD) // groups
    scale = jnp.exp2(ref[:, groups * height :, :].astype(jnp.float32)) * (1.0 / TOP)
    columns = []
    for group in range(groups):
        values = ref[:, group * height : (group + 1) * height, :].astype(jnp.float32)
        values = values * scale[:, group : group + 1, :]
        columns.append(values.astype(jnp.bfloat16).reshape(count * height, BLK))
    return jnp.concatenate(columns, axis=1)


def prepare(own, halves, rep_ref, tile_ref, right_ref, left_ref, tile, turned, arrived):
    rows = tile_ref.shape[0]
    copies = [
        pltpu.make_async_copy(
            tile_ref.at[pl.ds(part * own, own), :], tile.at[pl.ds(part * own, own), :], arrived.at[part]
        )
        for part in range(rows // own)
    ]
    for copy in copies:
        copy.start()
    for copy in copies:
        copy.wait()
    start = pl.multiple_of(rep_ref[0] * own, own)
    store_packed(right_ref, tile[pl.ds(start, own), :].astype(jnp.float32))
    turned[...] = tile[...].T
    for half in range(halves):
        piece = turned[pl.ds(pl.multiple_of(half * rows + start, own), own), :]
        for to in range(left_ref.shape[0]):
            left_ref[to, half * own : (half + 1) * own, :] = piece


def square_part(own, halves, packed_ref, left_ref, out_ref, right_ref):
    right_ref[...] = panel(packed_ref, right_ref.shape[1] // BLK)
    product = contract(right_ref[...], left_ref[...])
    rows = product.shape[0] // halves
    for rep in range(out_ref.shape[0]):
        for half in range(halves):
            first = half * rows + rep * own
            out_ref[rep, half * own : (half + 1) * own, :] = product[first : first + own, :]


def square_sum(own, halves, rep_ref, keep_ref, parts_ref, square_ref, low_ref):
    total = parts_ref[0]
    for rep in range(1, parts_ref.shape[0]):
        total = total + parts_ref[rep]
    rows = parts_ref.shape[2]
    per_half = rows // BLK
    start = rep_ref[0] * own
    for half in range(halves):
        block = lax.div(lax.broadcasted_iota(jnp.int32, (own, BLK), 0) + start, BLK)
        for across in range(rows // BLK):
            kept = jnp.zeros((own, BLK), jnp.float32)
            for down in range(per_half):
                keep = keep_ref[across, half * per_half + down].astype(jnp.float32)
                kept = jnp.where(block == down, keep, kept)
            at = slice(half * own, (half + 1) * own), slice(across * BLK, (across + 1) * BLK)
            square_ref[at] = total[at] * kept
    store_packed(low_ref, square_ref[...].astype(jnp.bfloat16).astype(jnp.float32))


def cube_part(own, halves, rep_ref, keep_ref, low_ref, right_ref, square_ref, out_ref, placed, total):
    rows, cols = total.shape
    start = pl.multiple_of(rep_ref[0] * own, own)
    placed[...] = jnp.zeros_like(placed)
    for half in range(halves):
        placed[pl.ds(pl.multiple_of(half * rows + start, own), own), :] = (
            3.0 * square_ref[half * own : (half + 1) * own, :]
        )
    product = contract(panel(low_ref, rows // BLK), right_ref[...])
    for down in range(rows // BLK):
        for across in range(cols // BLK):
            at = slice(down * BLK, (down + 1) * BLK), slice(across * BLK, (across + 1) * BLK)
            factor = -2.0 * keep_ref[down, across].astype(jnp.float32)
            total[at] = placed[at[1], at[0]].T + factor * product[at]
    for rep in range(out_ref.shape[0]):
        store_coded(out_ref.at[rep], total[rep * own : (rep + 1) * own, :])


def local(density, keep_square, keep_cube):
    rows, cols = density.shape
    reps, col_count = lax.axis_size("rep"), lax.axis_size("col")
    own, halves = rows // reps, cols // rows
    rep = lax.axis_index("rep").astype(jnp.int32).reshape(1)
    shape = jax.ShapeDtypeStruct
    part = halves * own

    right_coded, left_copies = call(
        functools.partial(prepare, own, halves),
        (
            shape((own * (cols // BLK) + HEAD, BLK), jnp.bfloat16),
            shape((col_count, part, rows), jnp.bfloat16),
        ),
        [SMEM, pl.BlockSpec(memory_space=pltpu.HBM)],
        [
            pltpu.VMEM((rows, cols), jnp.bfloat16),
            pltpu.VMEM((cols, rows), jnp.bfloat16),
            pltpu.SemaphoreType.DMA((reps,)),
        ],
    )(rep, pltpu.with_memory_space_constraint(density, pltpu.HBM))
    left = lax.all_to_all(left_copies, "col", 0, 0).reshape(col_count * part, rows)
    right = gather(right_coded, "row")
    parts, right = call(
        functools.partial(square_part, own, halves),
        (
            shape((reps, part, rows), jnp.float32),
            shape((right.shape[0] * own, cols), jnp.bfloat16),
        ),
        [VMEM, VMEM],
    )(right, left)
    parts = lax.all_to_all(parts, "rep", 0, 0)
    square, low_coded = call(
        functools.partial(square_sum, own, halves),
        (
            shape((part, rows), jnp.float32),
            shape((part * (rows // BLK) + HEAD, BLK), jnp.bfloat16),
        ),
        [SMEM, SMEM, VMEM],
    )(rep, keep_square, parts)
    low = gather(low_coded, "col")
    total = call(
        functools.partial(cube_part, own, halves),
        shape((reps, own + HEAD, cols), jnp.float32),
        [SMEM, SMEM, VMEM, VMEM, VMEM],
        [pltpu.VMEM((cols, rows), jnp.float32), pltpu.VMEM((rows, cols), jnp.float32)],
    )(rep, keep_cube, low, right, square)
    return jnp.sum(decode(lax.all_to_all(total.astype(jnp.float16), "rep", 0, 0)), axis=0)


def solution(mesh):
    return jax.shard_map(
        local,
        mesh=mesh,
        in_specs=(P("row", "col"), P("row", "col"), P("row", "col")),
        out_specs=P(("row", "rep"), "col"),
        check_vma=False,
    )
```

```python
import functools

import jax
import jax.numpy as jnp
from jax import lax
from jax.experimental import pallas as pl
from jax.experimental.pallas import tpu as pltpu
from jax.sharding import PartitionSpec as P

BLK = 128
TOP = 8192.0
LOWEST, HIGHEST = -100.0, 126.0
HEAD = 8

SMEM = pl.BlockSpec(memory_space=pltpu.SMEM)
VMEM = pl.BlockSpec(memory_space=pltpu.VMEM)
HBM = pl.BlockSpec(memory_space=pltpu.HBM)


def call(kernel, out_shape, in_specs, scratch=()):
    return pl.pallas_call(
        kernel,
        out_shape=out_shape,
        in_specs=in_specs,
        scratch_shapes=list(scratch),
        compiler_params=pltpu.CompilerParams(vmem_limit_bytes=32 << 20),
    )


def contract(a, b):
    return lax.dot_general(a, b, (((0,), (0,)), ((), ())), preferred_element_type=jnp.float32)


def scaled(values):
    largest = jnp.max(jnp.abs(values), axis=0, keepdims=True)
    exponent = jnp.floor(jnp.log2(jnp.maximum(largest, 2.0**LOWEST)))
    exponent = jnp.clip(exponent, LOWEST, HIGHEST)
    return values * jnp.exp2(-exponent) * TOP, exponent


def store_coded(ref, values):
    coded, exponent = scaled(values)
    height = values.shape[0]
    ref[:height, :] = coded.astype(ref.dtype)
    ref[height:, :] = jnp.broadcast_to(exponent, (HEAD, values.shape[1])).astype(ref.dtype)


def store_packed(ref, values):
    coded, exponent = scaled(values)
    height, width = values.shape
    groups = width // BLK
    for group in range(groups):
        columns = slice(group * BLK, (group + 1) * BLK)
        ref[group * height : (group + 1) * height, :] = coded[:, columns].astype(ref.dtype)
    rows = [exponent[:, group * BLK : (group + 1) * BLK] for group in range(groups)]
    rows.append(jnp.zeros((HEAD - groups, BLK), jnp.float32))
    ref[groups * height :, :] = jnp.concatenate(rows, axis=0).astype(ref.dtype)


def decode(pieces):
    height = pieces.shape[1] - HEAD
    scale = jnp.exp2(pieces[:, height : height + 1, :].astype(jnp.float32))
    return pieces[:, :height, :].astype(jnp.float32) * (1.0 / TOP) * scale


def gather(packed, axis):
    return lax.all_gather(packed.astype(jnp.float16), axis).astype(jnp.bfloat16)


def panel(ref, groups):
    count, height, _ = ref.shape
    height = (height - HEAD) // groups
    scale = jnp.exp2(ref[:, groups * height :, :].astype(jnp.float32)) * (1.0 / TOP)
    columns = []
    for group in range(groups):
        values = ref[:, group * height : (group + 1) * height, :].astype(jnp.float32)
        values = values * scale[:, group : group + 1, :]
        columns.append(values.astype(jnp.bfloat16).reshape(count * height, BLK))
    return jnp.concatenate(columns, axis=1)


def prepare(own, halves, rep_ref, tile_ref, right_ref, left_ref, tile, turned, arrived):
    rows = tile_ref.shape[0]
    copies = [
        pltpu.make_async_copy(
            tile_ref.at[pl.ds(part * own, own), :], tile.at[pl.ds(part * own, own), :], arrived.at[part]
        )
        for part in range(rows // own)
    ]
    for copy in copies:
        copy.start()
    for copy in copies:
        copy.wait()
    start = pl.multiple_of(rep_ref[0] * own, own)
    store_packed(right_ref, tile[pl.ds(start, own), :].astype(jnp.float32))
    turned[...] = tile[...].T
    for half in range(halves):
        piece = turned[pl.ds(pl.multiple_of(half * rows + start, own), own), :]
        for to in range(left_ref.shape[0]):
            left_ref[to, half * own : (half + 1) * own, :] = piece


def square_part(own, halves, packed_ref, left_ref, out_ref, right_ref, left, arrived):
    load = pltpu.make_async_copy(left_ref, left, arrived)
    load.start()
    right_ref[...] = panel(packed_ref, right_ref.shape[1] // BLK)
    load.wait()
    product = contract(right_ref[...], left[...])
    rows = product.shape[0] // halves
    for rep in range(out_ref.shape[0]):
        for half in range(halves):
            first = half * rows + rep * own
            out_ref[rep, half * own : (half + 1) * own, :] = product[first : first + own, :]


def square_sum(own, halves, rep_ref, keep_ref, later_ref, parts_ref, square_ref, low_ref, factor_ref):
    total = parts_ref[0]
    for rep in range(1, parts_ref.shape[0]):
        total = total + parts_ref[rep]
    rows = parts_ref.shape[2]
    per_half = rows // BLK
    start = rep_ref[0] * own
    for half in range(halves):
        block = lax.div(lax.broadcasted_iota(jnp.int32, (own, BLK), 0) + start, BLK)
        for across in range(rows // BLK):
            kept = jnp.zeros((own, BLK), jnp.float32)
            for down in range(per_half):
                keep = keep_ref[across, half * per_half + down].astype(jnp.float32)
                kept = jnp.where(block == down, keep, kept)
            at = slice(half * own, (half + 1) * own), slice(across * BLK, (across + 1) * BLK)
            square_ref[at] = total[at] * kept
    for down in range(later_ref.shape[0]):
        for across in range(later_ref.shape[1]):
            factor = -2.0 * later_ref[down, across].astype(jnp.float32)
            factor_ref[down, :, across * BLK : (across + 1) * BLK] = jnp.full((8, BLK), factor)
    store_packed(low_ref, square_ref[...].astype(jnp.bfloat16).astype(jnp.float32))


def cube_part(own, halves, rep_ref, factor_ref, low_ref, right_ref, square_ref, out_ref, placed, total):
    rows, cols = total.shape
    start = pl.multiple_of(rep_ref[0] * own, own)
    placed[...] = jnp.zeros_like(placed)
    for half in range(halves):
        placed[pl.ds(pl.multiple_of(half * rows + start, own), own), :] = (
            3.0 * square_ref[half * own : (half + 1) * own, :]
        )
    product = contract(panel(low_ref, rows // BLK), right_ref[...])
    for down in range(rows // BLK):
        for across in range(cols // BLK):
            at = slice(down * BLK, (down + 1) * BLK), slice(across * BLK, (across + 1) * BLK)
            total[at] = placed[at[1], at[0]].T + factor_ref[down, :1, at[1]] * product[at]
    for rep in range(out_ref.shape[0]):
        store_coded(out_ref.at[rep], total[rep * own : (rep + 1) * own, :])


def local(density, keep_square, keep_cube):
    rows, cols = density.shape
    reps, col_count = lax.axis_size("rep"), lax.axis_size("col")
    own, halves = rows // reps, cols // rows
    rep = lax.axis_index("rep").astype(jnp.int32).reshape(1)
    shape = jax.ShapeDtypeStruct
    part = halves * own

    right_coded, left_copies = call(
        functools.partial(prepare, own, halves),
        (
            shape((own * (cols // BLK) + HEAD, BLK), jnp.bfloat16),
            shape((col_count, part, rows), jnp.bfloat16),
        ),
        [SMEM, HBM],
        [
            pltpu.VMEM((rows, cols), jnp.bfloat16),
            pltpu.VMEM((cols, rows), jnp.bfloat16),
            pltpu.SemaphoreType.DMA((reps,)),
        ],
    )(rep, pltpu.with_memory_space_constraint(density, pltpu.HBM))
    left = lax.all_to_all(left_copies, "col", 0, 0).reshape(col_count * part, rows)
    left = pltpu.with_memory_space_constraint(left, pltpu.HBM)
    right = gather(right_coded, "row")
    parts, right = call(
        functools.partial(square_part, own, halves),
        (
            shape((reps, part, rows), jnp.float32),
            shape((right.shape[0] * own, cols), jnp.bfloat16),
        ),
        [VMEM, HBM],
        [pltpu.VMEM(left.shape, left.dtype), pltpu.SemaphoreType.DMA],
    )(right, left)
    parts = lax.all_to_all(parts, "rep", 0, 0)
    square, low_coded, factor = call(
        functools.partial(square_sum, own, halves),
        (
            shape((part, rows), jnp.float32),
            shape((part * (rows // BLK) + HEAD, BLK), jnp.bfloat16),
            shape((rows // BLK, 8, cols), jnp.float32),
        ),
        [SMEM, SMEM, SMEM, VMEM],
    )(rep, keep_square, keep_cube, parts)
    low = gather(low_coded, "col")
    total = call(
        functools.partial(cube_part, own, halves),
        shape((reps, own + HEAD, cols), jnp.float32),
        [SMEM, VMEM, VMEM, VMEM, VMEM],
        [pltpu.VMEM((cols, rows), jnp.float32), pltpu.VMEM((rows, cols), jnp.float32)],
    )(rep, factor, low, right, square)
    return jnp.sum(decode(lax.all_to_all(total.astype(jnp.float16), "rep", 0, 0)), axis=0)


def solution(mesh):
    return jax.shard_map(
        local,
        mesh=mesh,
        in_specs=(P("row", "col"), P("row", "col"), P("row", "col")),
        out_specs=P(("row", "rep"), "col"),
        check_vma=False,
    )
```

```python
import functools

import jax
import jax.numpy as jnp
from jax import lax
from jax.experimental import pallas as pl
from jax.experimental.pallas import tpu as pltpu
from jax.sharding import PartitionSpec as P

BLK = 128
TOP = 8192.0
LOWEST, HIGHEST = -100.0, 126.0
HEAD = 8

SMEM = pl.BlockSpec(memory_space=pltpu.SMEM)
VMEM = pl.BlockSpec(memory_space=pltpu.VMEM)
HBM = pl.BlockSpec(memory_space=pltpu.HBM)


def call(kernel, out_shape, in_specs, scratch=()):
    return pl.pallas_call(
        kernel,
        out_shape=out_shape,
        in_specs=in_specs,
        scratch_shapes=list(scratch),
        compiler_params=pltpu.CompilerParams(vmem_limit_bytes=32 << 20),
    )


def contract(a, b):
    return lax.dot_general(a, b, (((0,), (0,)), ((), ())), preferred_element_type=jnp.float32)


def scaled(values):
    largest = jnp.max(jnp.abs(values), axis=0, keepdims=True)
    exponent = jnp.floor(jnp.log2(jnp.maximum(largest, 2.0**LOWEST)))
    exponent = jnp.clip(exponent, LOWEST, HIGHEST)
    return values * jnp.exp2(-exponent) * TOP, exponent


def store_coded(ref, values):
    coded, exponent = scaled(values)
    height = values.shape[0]
    ref[:height, :] = coded.astype(ref.dtype)
    ref[height:, :] = jnp.broadcast_to(exponent, (HEAD, values.shape[1])).astype(ref.dtype)


def store_packed(ref, values):
    coded, exponent = scaled(values)
    height, width = values.shape
    groups = width // BLK
    for group in range(groups):
        columns = slice(group * BLK, (group + 1) * BLK)
        ref[group * height : (group + 1) * height, :] = coded[:, columns].astype(ref.dtype)
    rows = [exponent[:, group * BLK : (group + 1) * BLK] for group in range(groups)]
    rows.append(jnp.zeros((HEAD - groups, BLK), jnp.float32))
    ref[groups * height :, :] = jnp.concatenate(rows, axis=0).astype(ref.dtype)


def decode(pieces):
    height = pieces.shape[1] - HEAD
    scale = jnp.exp2(pieces[:, height : height + 1, :].astype(jnp.float32))
    return pieces[:, :height, :].astype(jnp.float32) * (1.0 / TOP) * scale


def gather(packed, axis, groups):
    whole = lax.all_gather(packed.astype(jnp.float16), axis)
    count, height = whole.shape[0], whole.shape[1] - HEAD
    scale = jnp.exp2(whole[:, height : height + groups, :].astype(jnp.float32)) * (1.0 / TOP)
    scale = jnp.broadcast_to(scale[:, :, None, :], (count, groups, height // groups, BLK))
    values = whole[:, :height, :].astype(jnp.float32) * scale.reshape(count, height, BLK)
    return values.astype(jnp.bfloat16)


def panel(ref, groups):
    count, height, _ = ref.shape
    height //= groups
    columns = [
        ref[:, group * height : (group + 1) * height, :].reshape(count * height, BLK)
        for group in range(groups)
    ]
    return jnp.concatenate(columns, axis=1)


def prepare(own, halves, rep_ref, tile_ref, right_ref, left_ref, tile, turned, arrived):
    rows = tile_ref.shape[0]
    copies = [
        pltpu.make_async_copy(
            tile_ref.at[pl.ds(part * own, own), :], tile.at[pl.ds(part * own, own), :], arrived.at[part]
        )
        for part in range(rows // own)
    ]
    for copy in copies:
        copy.start()
    for copy in copies:
        copy.wait()
    start = pl.multiple_of(rep_ref[0] * own, own)
    store_packed(right_ref, tile[pl.ds(start, own), :].astype(jnp.float32))
    turned[...] = tile[...].T
    for half in range(halves):
        piece = turned[pl.ds(pl.multiple_of(half * rows + start, own), own), :]
        for to in range(left_ref.shape[0]):
            left_ref[to, half * own : (half + 1) * own, :] = piece


def square_part(own, halves, right_ref, left_ref, out_ref):
    product = contract(panel(right_ref, right_ref.shape[1] // own), left_ref[...])
    rows = product.shape[0] // halves
    for rep in range(out_ref.shape[0]):
        for half in range(halves):
            first = half * rows + rep * own
            out_ref[rep, half * own : (half + 1) * own, :] = product[first : first + own, :]


def square_sum(own, halves, rep_ref, keep_ref, later_ref, parts_ref, square_ref, low_ref, factor_ref):
    total = parts_ref[0]
    for rep in range(1, parts_ref.shape[0]):
        total = total + parts_ref[rep]
    rows = parts_ref.shape[2]
    per_half = rows // BLK
    start = rep_ref[0] * own
    for half in range(halves):
        block = lax.div(lax.broadcasted_iota(jnp.int32, (own, BLK), 0) + start, BLK)
        for across in range(rows // BLK):
            kept = jnp.zeros((own, BLK), jnp.float32)
            for down in range(per_half):
                keep = keep_ref[across, half * per_half + down].astype(jnp.float32)
                kept = jnp.where(block == down, keep, kept)
            at = slice(half * own, (half + 1) * own), slice(across * BLK, (across + 1) * BLK)
            square_ref[at] = total[at] * kept
    for down in range(later_ref.shape[0]):
        for across in range(later_ref.shape[1]):
            factor = -2.0 * later_ref[down, across].astype(jnp.float32)
            factor_ref[down, :, across * BLK : (across + 1) * BLK] = jnp.full((8, BLK), factor)
    store_packed(low_ref, square_ref[...].astype(jnp.bfloat16).astype(jnp.float32))


def cube_part(own, halves, rep_ref, factor_ref, low_ref, right_ref, square_ref, out_ref, placed, total):
    rows, cols = total.shape
    start = pl.multiple_of(rep_ref[0] * own, own)
    placed[...] = jnp.zeros_like(placed)
    for half in range(halves):
        placed[pl.ds(pl.multiple_of(half * rows + start, own), own), :] = (
            3.0 * square_ref[half * own : (half + 1) * own, :]
        )
    product = contract(panel(low_ref, rows // BLK), panel(right_ref, cols // BLK))
    for down in range(rows // BLK):
        for across in range(cols // BLK):
            at = slice(down * BLK, (down + 1) * BLK), slice(across * BLK, (across + 1) * BLK)
            total[at] = placed[at[1], at[0]].T + factor_ref[down, :1, at[1]] * product[at]
    for rep in range(out_ref.shape[0]):
        store_coded(out_ref.at[rep], total[rep * own : (rep + 1) * own, :])


def local(density, keep_square, keep_cube):
    rows, cols = density.shape
    reps, col_count = lax.axis_size("rep"), lax.axis_size("col")
    own, halves = rows // reps, cols // rows
    rep = lax.axis_index("rep").astype(jnp.int32).reshape(1)
    shape = jax.ShapeDtypeStruct
    part = halves * own

    right_coded, left_copies = call(
        functools.partial(prepare, own, halves),
        (
            shape((own * (cols // BLK) + HEAD, BLK), jnp.bfloat16),
            shape((col_count, part, rows), jnp.bfloat16),
        ),
        [SMEM, HBM],
        [
            pltpu.VMEM((rows, cols), jnp.bfloat16),
            pltpu.VMEM((cols, rows), jnp.bfloat16),
            pltpu.SemaphoreType.DMA((reps,)),
        ],
    )(rep, pltpu.with_memory_space_constraint(density, pltpu.HBM))
    left = lax.all_to_all(left_copies, "col", 0, 0).reshape(col_count * part, rows)
    right = gather(right_coded, "row", cols // BLK)
    parts = call(
        functools.partial(square_part, own, halves),
        shape((reps, part, rows), jnp.float32),
        [VMEM, VMEM],
    )(right, left)
    parts = lax.all_to_all(parts, "rep", 0, 0)
    square, low_coded, factor = call(
        functools.partial(square_sum, own, halves),
        (
            shape((part, rows), jnp.float32),
            shape((part * (rows // BLK) + HEAD, BLK), jnp.bfloat16),
            shape((rows // BLK, 8, cols), jnp.float32),
        ),
        [SMEM, SMEM, SMEM, VMEM],
    )(rep, keep_square, keep_cube, parts)
    low = gather(low_coded, "col", rows // BLK)
    total = call(
        functools.partial(cube_part, own, halves),
        shape((reps, own + HEAD, cols), jnp.float32),
        [SMEM, VMEM, VMEM, VMEM, VMEM],
        [pltpu.VMEM((cols, rows), jnp.float32), pltpu.VMEM((rows, cols), jnp.float32)],
    )(rep, factor, low, right, square)
    return jnp.sum(decode(lax.all_to_all(total.astype(jnp.float16), "rep", 0, 0)), axis=0)


def solution(mesh):
    return jax.shard_map(
        local,
        mesh=mesh,
        in_specs=(P("row", "col"), P("row", "col"), P("row", "col")),
        out_specs=P(("row", "rep"), "col"),
        check_vma=False,
    )
```

```python
import functools

import jax
import jax.numpy as jnp
from jax import lax
from jax.experimental import pallas as pl
from jax.experimental.pallas import tpu as pltpu
from jax.sharding import PartitionSpec as P

BLK = 128
TOP = 8192.0
LOWEST, HIGHEST = -100.0, 126.0
HEAD = 8

SMEM = pl.BlockSpec(memory_space=pltpu.SMEM)
VMEM = pl.BlockSpec(memory_space=pltpu.VMEM)
HBM = pl.BlockSpec(memory_space=pltpu.HBM)


def call(kernel, out_shape, in_specs, scratch=()):
    return pl.pallas_call(
        kernel,
        out_shape=out_shape,
        in_specs=in_specs,
        scratch_shapes=list(scratch),
        compiler_params=pltpu.CompilerParams(vmem_limit_bytes=32 << 20),
    )


def contract(a, b):
    return lax.dot_general(a, b, (((0,), (0,)), ((), ())), preferred_element_type=jnp.float32)


def scaled(values):
    largest = jnp.max(jnp.abs(values), axis=0, keepdims=True)
    exponent = jnp.floor(jnp.log2(jnp.maximum(largest, 2.0**LOWEST)))
    exponent = jnp.clip(exponent, LOWEST, HIGHEST)
    return values * jnp.exp2(-exponent) * TOP, exponent


def store_coded(ref, values):
    coded, exponent = scaled(values)
    height = values.shape[0]
    ref[:height, :] = coded.astype(ref.dtype)
    ref[height:, :] = jnp.broadcast_to(exponent, (HEAD, values.shape[1])).astype(ref.dtype)


def store_packed(ref, values):
    coded, exponent = scaled(values)
    height, width = values.shape
    groups = width // BLK
    for group in range(groups):
        columns = slice(group * BLK, (group + 1) * BLK)
        ref[group * height : (group + 1) * height, :] = coded[:, columns].astype(ref.dtype)
    rows = [exponent[:, group * BLK : (group + 1) * BLK] for group in range(groups)]
    rows.append(jnp.zeros((HEAD - groups, BLK), jnp.float32))
    ref[groups * height :, :] = jnp.concatenate(rows, axis=0).astype(ref.dtype)


def decode(pieces):
    height = pieces.shape[1] - HEAD
    scale = jnp.exp2(pieces[:, height : height + 1, :].astype(jnp.float32))
    return pieces[:, :height, :].astype(jnp.float32) * (1.0 / TOP) * scale


def gather(packed, axis, groups):
    whole = lax.all_gather(packed.astype(jnp.float16), axis)
    count, height = whole.shape[0], whole.shape[1] - HEAD
    scale = jnp.exp2(whole[:, height : height + groups, :].astype(jnp.float32)) * (1.0 / TOP)
    scale = jnp.broadcast_to(scale[:, :, None, :], (count, groups, height // groups, BLK))
    values = whole[:, :height, :].astype(jnp.float32) * scale.reshape(count, height, BLK)
    return values.astype(jnp.bfloat16)


def panel(ref, groups):
    count, height, _ = ref.shape
    height //= groups
    columns = [
        ref[:, group * height : (group + 1) * height, :].reshape(count * height, BLK)
        for group in range(groups)
    ]
    return jnp.concatenate(columns, axis=1)


def window_start(start, rows, width):
    return pl.multiple_of(jnp.minimum(lax.div(start, BLK) * BLK, rows - width), BLK)


def prepare(own, halves, rep_ref, tile_ref, right_ref, left_ref, tile, turned, arrived):
    rows = tile_ref.shape[0]
    copies = [
        pltpu.make_async_copy(
            tile_ref.at[pl.ds(part * own, own), :], tile.at[pl.ds(part * own, own), :], arrived.at[part]
        )
        for part in range(rows // own)
    ]
    for copy in copies:
        copy.start()
    for copy in copies:
        copy.wait()
    start = pl.multiple_of(rep_ref[0] * own, own)
    store_packed(right_ref, tile[pl.ds(start, own), :].astype(jnp.float32))
    width = turned.shape[0]
    first = window_start(start, rows, width)
    for half in range(halves):
        turned[...] = tile[:, pl.ds(pl.multiple_of(half * rows + first, BLK), width)].T
        piece = turned[pl.ds(pl.multiple_of(start - first, 16), own), :]
        for to in range(left_ref.shape[0]):
            left_ref[to, half * own : (half + 1) * own, :] = piece


def square_part(own, halves, right_ref, left_ref, out_ref):
    product = contract(left_ref[...], panel(right_ref, right_ref.shape[1] // own)).T
    rows = product.shape[0] // halves
    for rep in range(out_ref.shape[0]):
        for half in range(halves):
            first = half * rows + rep * own
            out_ref[rep, half * own : (half + 1) * own, :] = product[first : first + own, :]


def square_sum(own, halves, rep_ref, keep_ref, later_ref, parts_ref, square_ref, low_ref, factor_ref):
    total = parts_ref[0]
    for rep in range(1, parts_ref.shape[0]):
        total = total + parts_ref[rep]
    rows = parts_ref.shape[2]
    per_half = rows // BLK
    start = rep_ref[0] * own
    for half in range(halves):
        block = lax.div(lax.broadcasted_iota(jnp.int32, (own, BLK), 0) + start, BLK)
        for across in range(rows // BLK):
            kept = jnp.zeros((own, BLK), jnp.float32)
            for down in range(per_half):
                keep = keep_ref[across, half * per_half + down].astype(jnp.float32)
                kept = jnp.where(block == down, keep, kept)
            at = slice(half * own, (half + 1) * own), slice(across * BLK, (across + 1) * BLK)
            square_ref[at] = total[at] * kept
    for down in range(later_ref.shape[0]):
        for across in range(later_ref.shape[1]):
            factor = -2.0 * later_ref[down, across].astype(jnp.float32)
            factor_ref[down, :, across * BLK : (across + 1) * BLK] = jnp.full((8, BLK), factor)
    store_packed(low_ref, square_ref[...].astype(jnp.bfloat16).astype(jnp.float32))


def cube_part(own, halves, rep_ref, factor_ref, low_ref, right_ref, square_ref, out_ref, placed, total):
    rows, cols = total.shape
    width = placed.shape[0]
    start = pl.multiple_of(rep_ref[0] * own, own)
    first = window_start(start, rows, width)
    product = contract(panel(low_ref, rows // BLK), panel(right_ref, cols // BLK))
    for down in range(rows // BLK):
        for across in range(cols // BLK):
            at = slice(down * BLK, (down + 1) * BLK), slice(across * BLK, (across + 1) * BLK)
            total[at] = factor_ref[down, :1, at[1]] * product[at]
    placed[...] = jnp.zeros_like(placed)
    for half in range(halves):
        placed[pl.ds(pl.multiple_of(start - first, 8), own), :] = (
            3.0 * square_ref[half * own : (half + 1) * own, :]
        )
        columns = pl.ds(pl.multiple_of(half * rows + first, BLK), width)
        total[:, columns] = placed[...].T + total[:, columns]
    for rep in range(out_ref.shape[0]):
        store_coded(out_ref.at[rep], total[rep * own : (rep + 1) * own, :])


def local(density, keep_square, keep_cube):
    rows, cols = density.shape
    reps, col_count = lax.axis_size("rep"), lax.axis_size("col")
    own, halves = rows // reps, cols // rows
    rep = lax.axis_index("rep").astype(jnp.int32).reshape(1)
    shape = jax.ShapeDtypeStruct
    part = halves * own
    width = -(-own // BLK) * BLK + BLK

    right_coded, left_copies = call(
        functools.partial(prepare, own, halves),
        (
            shape((own * (cols // BLK) + HEAD, BLK), jnp.bfloat16),
            shape((col_count, part, rows), jnp.bfloat16),
        ),
        [SMEM, HBM],
        [
            pltpu.VMEM((rows, cols), jnp.bfloat16),
            pltpu.VMEM((width, rows), jnp.bfloat16),
            pltpu.SemaphoreType.DMA((reps,)),
        ],
    )(rep, pltpu.with_memory_space_constraint(density, pltpu.HBM))
    left = lax.all_to_all(left_copies, "col", 0, 0).reshape(col_count * part, rows)
    right = gather(right_coded, "row", cols // BLK)
    parts = call(
        functools.partial(square_part, own, halves),
        shape((reps, part, rows), jnp.float32),
        [VMEM, VMEM],
    )(right, left)
    parts = lax.all_to_all(parts, "rep", 0, 0)
    square, low_coded, factor = call(
        functools.partial(square_sum, own, halves),
        (
            shape((part, rows), jnp.float32),
            shape((part * (rows // BLK) + HEAD, BLK), jnp.bfloat16),
            shape((rows // BLK, 8, cols), jnp.float32),
        ),
        [SMEM, SMEM, SMEM, VMEM],
    )(rep, keep_square, keep_cube, parts)
    low = gather(low_coded, "col", rows // BLK)
    total = call(
        functools.partial(cube_part, own, halves),
        shape((reps, own + HEAD, cols), jnp.float32),
        [SMEM, VMEM, VMEM, VMEM, VMEM],
        [pltpu.VMEM((width, rows), jnp.float32), pltpu.VMEM((rows, cols), jnp.float32)],
    )(rep, factor, low, right, square)
    return jnp.sum(decode(lax.all_to_all(total.astype(jnp.float16), "rep", 0, 0)), axis=0)


def solution(mesh):
    return jax.shard_map(
        local,
        mesh=mesh,
        in_specs=(P("row", "col"), P("row", "col"), P("row", "col")),
        out_specs=P(("row", "rep"), "col"),
        check_vma=False,
    )
```

```python
import functools

import jax
import jax.numpy as jnp
from jax import lax
from jax.experimental import pallas as pl
from jax.experimental.pallas import tpu as pltpu
from jax.sharding import PartitionSpec as P

BLK = 128
TOP = 8192.0
LOWEST, HIGHEST = -100.0, 126.0
HEAD = 8

SMEM = pl.BlockSpec(memory_space=pltpu.SMEM)
VMEM = pl.BlockSpec(memory_space=pltpu.VMEM)
HBM = pl.BlockSpec(memory_space=pltpu.HBM)


def call(kernel, out_shape, in_specs, scratch=()):
    return pl.pallas_call(
        kernel,
        out_shape=out_shape,
        in_specs=in_specs,
        scratch_shapes=list(scratch),
        compiler_params=pltpu.CompilerParams(vmem_limit_bytes=32 << 20),
    )


def contract(a, b):
    return lax.dot_general(a, b, (((0,), (0,)), ((), ())), preferred_element_type=jnp.float32)


def scaled(values):
    largest = jnp.max(jnp.abs(values), axis=0, keepdims=True)
    exponent = jnp.floor(jnp.log2(jnp.maximum(largest, 2.0**LOWEST)))
    exponent = jnp.clip(exponent, LOWEST, HIGHEST)
    return values * jnp.exp2(-exponent) * TOP, exponent


def store_coded(ref, values):
    coded, exponent = scaled(values)
    height = values.shape[0]
    ref[:height, :] = coded.astype(ref.dtype)
    ref[height:, :] = jnp.broadcast_to(exponent, (HEAD, values.shape[1])).astype(ref.dtype)


def store_packed(ref, values):
    coded, exponent = scaled(values)
    height, width = values.shape
    groups = width // BLK
    for group in range(groups):
        columns = slice(group * BLK, (group + 1) * BLK)
        ref[group * height : (group + 1) * height, :] = coded[:, columns].astype(ref.dtype)
    rows = [exponent[:, group * BLK : (group + 1) * BLK] for group in range(groups)]
    rows.append(jnp.zeros((HEAD - groups, BLK), jnp.float32))
    ref[groups * height :, :] = jnp.concatenate(rows, axis=0).astype(ref.dtype)


def decode(pieces):
    height = pieces.shape[1] - HEAD
    scale = jnp.exp2(pieces[:, height : height + 1, :].astype(jnp.float32))
    return pieces[:, :height, :].astype(jnp.float32) * (1.0 / TOP) * scale


def gather(packed, axis, groups):
    whole = lax.all_gather(packed.astype(jnp.float16), axis)
    count, height = whole.shape[0], whole.shape[1] - HEAD
    scale = jnp.exp2(whole[:, height : height + groups, :].astype(jnp.float32)) * (1.0 / TOP)
    scale = jnp.broadcast_to(scale[:, :, None, :], (count, groups, height // groups, BLK))
    values = whole[:, :height, :].astype(jnp.float32) * scale.reshape(count, height, BLK)
    return values.astype(jnp.bfloat16)


def panel(ref, groups):
    count, height, _ = ref.shape
    height //= groups
    columns = [
        ref[:, group * height : (group + 1) * height, :].reshape(count * height, BLK)
        for group in range(groups)
    ]
    return jnp.concatenate(columns, axis=1)


def window_start(start, rows, width):
    return pl.multiple_of(jnp.minimum(lax.div(start, BLK) * BLK, rows - width), BLK)


def prepare(own, halves, rep_ref, tile_ref, right_ref, left_ref, tile, turned, arrived):
    rows = tile_ref.shape[0]
    copies = [
        pltpu.make_async_copy(
            tile_ref.at[pl.ds(part * own, own), :], tile.at[pl.ds(part * own, own), :], arrived.at[part]
        )
        for part in range(rows // own)
    ]
    for copy in copies:
        copy.start()
    for copy in copies:
        copy.wait()
    start = pl.multiple_of(rep_ref[0] * own, own)
    store_packed(right_ref, tile[pl.ds(start, own), :].astype(jnp.float32))
    width = turned.shape[0]
    first = window_start(start, rows, width)
    for half in range(halves):
        turned[...] = tile[:, pl.ds(pl.multiple_of(half * rows + first, BLK), width)].T
        piece = turned[pl.ds(pl.multiple_of(start - first, 16), own), :]
        for to in range(left_ref.shape[0]):
            left_ref[to, half * own : (half + 1) * own, :] = piece


def square_part(own, halves, right_ref, left_ref, out_ref):
    product = contract(left_ref[...], panel(right_ref, right_ref.shape[1] // own)).T
    rows = product.shape[0] // halves
    for rep in range(out_ref.shape[0]):
        for half in range(halves):
            first = half * rows + rep * own
            out_ref[rep, half * own : (half + 1) * own, :] = product[first : first + own, :]


def square_sum(own, halves, rep_ref, keep_ref, later_ref, parts_ref, square_ref, low_ref, factor_ref):
    total = parts_ref[0]
    for rep in range(1, parts_ref.shape[0]):
        total = total + parts_ref[rep]
    rows = parts_ref.shape[2]
    per_half = rows // BLK
    start = rep_ref[0] * own
    for half in range(halves):
        block = lax.div(lax.broadcasted_iota(jnp.int32, (own, BLK), 0) + start, BLK)
        for across in range(rows // BLK):
            kept = jnp.zeros((own, BLK), jnp.float32)
            for down in range(per_half):
                keep = keep_ref[across, half * per_half + down].astype(jnp.float32)
                kept = jnp.where(block == down, keep, kept)
            at = slice(half * own, (half + 1) * own), slice(across * BLK, (across + 1) * BLK)
            square_ref[at] = total[at] * kept
    for down in range(later_ref.shape[0]):
        for across in range(later_ref.shape[1]):
            factor = -2.0 * later_ref[down, across].astype(jnp.float32)
            factor_ref[down, :, across * BLK : (across + 1) * BLK] = jnp.full((8, BLK), factor)
    store_packed(low_ref, square_ref[...].astype(jnp.bfloat16).astype(jnp.float32))


def cube_part(own, halves, rep_ref, factor_ref, low_ref, right_ref, square_ref, out_ref, placed, total):
    rows, cols = total.shape
    start = pl.multiple_of(rep_ref[0] * own, own)
    placed[...] = jnp.zeros_like(placed)
    for half in range(halves):
        placed[pl.ds(pl.multiple_of(half * rows + start, own), own), :] = (
            3.0 * square_ref[half * own : (half + 1) * own, :]
        )
    product = contract(panel(low_ref, rows // BLK), panel(right_ref, cols // BLK))
    for down in range(rows // BLK):
        for across in range(cols // BLK):
            at = slice(down * BLK, (down + 1) * BLK), slice(across * BLK, (across + 1) * BLK)
            total[at] = placed[at[1], at[0]].T + factor_ref[down, :1, at[1]] * product[at]
    for rep in range(out_ref.shape[0]):
        store_coded(out_ref.at[rep], total[rep * own : (rep + 1) * own, :])


def local(density, keep_square, keep_cube):
    rows, cols = density.shape
    reps, col_count = lax.axis_size("rep"), lax.axis_size("col")
    own, halves = rows // reps, cols // rows
    rep = lax.axis_index("rep").astype(jnp.int32).reshape(1)
    shape = jax.ShapeDtypeStruct
    part = halves * own
    width = -(-own // BLK) * BLK + BLK

    right_coded, left_copies = call(
        functools.partial(prepare, own, halves),
        (
            shape((own * (cols // BLK) + HEAD, BLK), jnp.bfloat16),
            shape((col_count, part, rows), jnp.bfloat16),
        ),
        [SMEM, HBM],
        [
            pltpu.VMEM((rows, cols), jnp.bfloat16),
            pltpu.VMEM((width, rows), jnp.bfloat16),
            pltpu.SemaphoreType.DMA((reps,)),
        ],
    )(rep, pltpu.with_memory_space_constraint(density, pltpu.HBM))
    left = lax.all_to_all(left_copies, "col", 0, 0).reshape(col_count * part, rows)
    right = gather(right_coded, "row", cols // BLK)
    parts = call(
        functools.partial(square_part, own, halves),
        shape((reps, part, rows), jnp.float32),
        [VMEM, VMEM],
    )(right, left)
    parts = lax.all_to_all(parts, "rep", 0, 0)
    square, low_coded, factor = call(
        functools.partial(square_sum, own, halves),
        (
            shape((part, rows), jnp.float32),
            shape((part * (rows // BLK) + HEAD, BLK), jnp.bfloat16),
            shape((rows // BLK, 8, cols), jnp.float32),
        ),
        [SMEM, SMEM, SMEM, VMEM],
    )(rep, keep_square, keep_cube, parts)
    low = gather(low_coded, "col", rows // BLK)
    total = call(
        functools.partial(cube_part, own, halves),
        shape((reps, own + HEAD, cols), jnp.float32),
        [SMEM, VMEM, VMEM, VMEM, VMEM],
        [pltpu.VMEM((cols, rows), jnp.float32), pltpu.VMEM((rows, cols), jnp.float32)],
    )(rep, factor, low, right, square)
    return jnp.sum(decode(lax.all_to_all(total.astype(jnp.float16), "rep", 0, 0)), axis=0)


def solution(mesh):
    return jax.shard_map(
        local,
        mesh=mesh,
        in_specs=(P("row", "col"), P("row", "col"), P("row", "col")),
        out_specs=P(("row", "rep"), "col"),
        check_vma=False,
    )
```

```python
import functools

import jax
import jax.numpy as jnp
from jax import lax
from jax.experimental import pallas as pl
from jax.experimental.pallas import tpu as pltpu
from jax.sharding import PartitionSpec as P

BLK = 128
TOP = 8192.0
LOWEST, HIGHEST = -100.0, 126.0
HEAD = 8

SMEM = pl.BlockSpec(memory_space=pltpu.SMEM)
VMEM = pl.BlockSpec(memory_space=pltpu.VMEM)
HBM = pl.BlockSpec(memory_space=pltpu.HBM)


def call(kernel, out_shape, in_specs, scratch=()):
    return pl.pallas_call(
        kernel,
        out_shape=out_shape,
        in_specs=in_specs,
        scratch_shapes=list(scratch),
        compiler_params=pltpu.CompilerParams(vmem_limit_bytes=32 << 20),
    )


def contract(a, b):
    return lax.dot_general(a, b, (((0,), (0,)), ((), ())), preferred_element_type=jnp.float32)


def scaled(values):
    largest = jnp.max(jnp.abs(values), axis=0, keepdims=True)
    exponent = jnp.floor(jnp.log2(jnp.maximum(largest, 2.0**LOWEST)))
    exponent = jnp.clip(exponent, LOWEST, HIGHEST)
    return values * jnp.exp2(-exponent) * TOP, exponent


def store_coded(ref, values):
    coded, exponent = scaled(values)
    height = values.shape[0]
    ref[:height, :] = coded.astype(ref.dtype)
    ref[height:, :] = jnp.broadcast_to(exponent, (HEAD, values.shape[1])).astype(ref.dtype)


def store_packed(ref, values):
    coded, exponent = scaled(values)
    height, width = values.shape
    groups = width // BLK
    for group in range(groups):
        columns = slice(group * BLK, (group + 1) * BLK)
        ref[group * height : (group + 1) * height, :] = coded[:, columns].astype(ref.dtype)
    rows = [exponent[:, group * BLK : (group + 1) * BLK] for group in range(groups)]
    rows.append(jnp.zeros((HEAD - groups, BLK), jnp.float32))
    ref[groups * height :, :] = jnp.concatenate(rows, axis=0).astype(ref.dtype)


def decode(pieces):
    count, height, width = pieces.shape
    height -= HEAD
    scale = jnp.exp2(pieces[:, height:, :].astype(jnp.float32)) * (1.0 / TOP)
    scale = jnp.broadcast_to(scale[:, None], (count, height // HEAD, HEAD, width))
    return pieces[:, :height, :].astype(jnp.float32) * scale.reshape(count, height, width)


def gather(packed, axis, groups):
    whole = lax.all_gather(packed.astype(jnp.float16), axis)
    count, height = whole.shape[0], whole.shape[1] - HEAD
    scale = jnp.exp2(whole[:, height : height + groups, :].astype(jnp.float32)) * (1.0 / TOP)
    scale = jnp.broadcast_to(scale[:, :, None, :], (count, groups, height // groups, BLK))
    values = whole[:, :height, :].astype(jnp.float32) * scale.reshape(count, height, BLK)
    return values.astype(jnp.bfloat16)


def panel(ref, groups):
    count, height, _ = ref.shape
    height //= groups
    columns = [
        ref[:, group * height : (group + 1) * height, :].reshape(count * height, BLK)
        for group in range(groups)
    ]
    return jnp.concatenate(columns, axis=1)


def window_start(start, rows, width):
    return pl.multiple_of(jnp.minimum(lax.div(start, BLK) * BLK, rows - width), BLK)


def prepare(own, halves, rep_ref, tile_ref, right_ref, left_ref, tile, turned, arrived):
    rows = tile_ref.shape[0]
    copies = [
        pltpu.make_async_copy(
            tile_ref.at[pl.ds(part * own, own), :], tile.at[pl.ds(part * own, own), :], arrived.at[part]
        )
        for part in range(rows // own)
    ]
    for copy in copies:
        copy.start()
    for copy in copies:
        copy.wait()
    start = pl.multiple_of(rep_ref[0] * own, own)
    store_packed(right_ref, tile[pl.ds(start, own), :].astype(jnp.float32))
    width = turned.shape[0]
    first = window_start(start, rows, width)
    for half in range(halves):
        turned[...] = tile[:, pl.ds(pl.multiple_of(half * rows + first, BLK), width)].T
        piece = turned[pl.ds(pl.multiple_of(start - first, 16), own), :]
        for to in range(left_ref.shape[0]):
            left_ref[to, half * own : (half + 1) * own, :] = piece


def square_part(own, halves, right_ref, left_ref, out_ref):
    product = contract(left_ref[...], panel(right_ref, right_ref.shape[1] // own)).T
    rows = product.shape[0] // halves
    for rep in range(out_ref.shape[0]):
        for half in range(halves):
            first = half * rows + rep * own
            out_ref[rep, half * own : (half + 1) * own, :] = product[first : first + own, :]


def square_sum(own, halves, rep_ref, keep_ref, later_ref, parts_ref, square_ref, low_ref, factor_ref):
    total = parts_ref[0]
    for rep in range(1, parts_ref.shape[0]):
        total = total + parts_ref[rep]
    rows = parts_ref.shape[2]
    per_half = rows // BLK
    start = rep_ref[0] * own
    for half in range(halves):
        block = lax.div(lax.broadcasted_iota(jnp.int32, (own, BLK), 0) + start, BLK)
        for across in range(rows // BLK):
            kept = jnp.zeros((own, BLK), jnp.float32)
            for down in range(per_half):
                keep = keep_ref[across, half * per_half + down].astype(jnp.float32)
                kept = jnp.where(block == down, keep, kept)
            at = slice(half * own, (half + 1) * own), slice(across * BLK, (across + 1) * BLK)
            square_ref[at] = total[at] * kept
    for down in range(later_ref.shape[0]):
        for across in range(later_ref.shape[1]):
            factor = -2.0 * later_ref[down, across].astype(jnp.float32)
            factor_ref[down, :, across * BLK : (across + 1) * BLK] = jnp.full((8, BLK), factor)
    store_packed(low_ref, square_ref[...].astype(jnp.bfloat16).astype(jnp.float32))


def cube_part(own, halves, rep_ref, factor_ref, low_ref, right_ref, square_ref, out_ref, placed, total):
    rows, cols = total.shape
    start = pl.multiple_of(rep_ref[0] * own, own)
    placed[...] = jnp.zeros_like(placed)
    for half in range(halves):
        placed[pl.ds(pl.multiple_of(half * rows + start, own), own), :] = (
            3.0 * square_ref[half * own : (half + 1) * own, :]
        )
    product = contract(panel(low_ref, rows // BLK), panel(right_ref, cols // BLK))
    for down in range(rows // BLK):
        for across in range(cols // BLK):
            at = slice(down * BLK, (down + 1) * BLK), slice(across * BLK, (across + 1) * BLK)
            total[at] = placed[at[1], at[0]].T + factor_ref[down, :1, at[1]] * product[at]
    for rep in range(out_ref.shape[0]):
        store_coded(out_ref.at[rep], total[rep * own : (rep + 1) * own, :])


def local(density, keep_square, keep_cube):
    rows, cols = density.shape
    reps, col_count = lax.axis_size("rep"), lax.axis_size("col")
    own, halves = rows // reps, cols // rows
    rep = lax.axis_index("rep").astype(jnp.int32).reshape(1)
    shape = jax.ShapeDtypeStruct
    part = halves * own
    width = -(-own // BLK) * BLK + BLK

    right_coded, left_copies = call(
        functools.partial(prepare, own, halves),
        (
            shape((own * (cols // BLK) + HEAD, BLK), jnp.bfloat16),
            shape((col_count, part, rows), jnp.bfloat16),
        ),
        [SMEM, HBM],
        [
            pltpu.VMEM((rows, cols), jnp.bfloat16),
            pltpu.VMEM((width, rows), jnp.bfloat16),
            pltpu.SemaphoreType.DMA((reps,)),
        ],
    )(rep, pltpu.with_memory_space_constraint(density, pltpu.HBM))
    left = lax.all_to_all(left_copies, "col", 0, 0).reshape(col_count * part, rows)
    right = gather(right_coded, "row", cols // BLK)
    parts = call(
        functools.partial(square_part, own, halves),
        shape((reps, part, rows), jnp.float32),
        [VMEM, VMEM],
    )(right, left)
    parts = lax.all_to_all(parts, "rep", 0, 0)
    square, low_coded, factor = call(
        functools.partial(square_sum, own, halves),
        (
            shape((part, rows), jnp.float32),
            shape((part * (rows // BLK) + HEAD, BLK), jnp.bfloat16),
            shape((rows // BLK, 8, cols), jnp.float32),
        ),
        [SMEM, SMEM, SMEM, VMEM],
    )(rep, keep_square, keep_cube, parts)
    low = gather(low_coded, "col", rows // BLK)
    total = call(
        functools.partial(cube_part, own, halves),
        shape((reps, own + HEAD, cols), jnp.float32),
        [SMEM, VMEM, VMEM, VMEM, VMEM],
        [pltpu.VMEM((cols, rows), jnp.float32), pltpu.VMEM((rows, cols), jnp.float32)],
    )(rep, factor, low, right, square)
    return jnp.sum(decode(lax.all_to_all(total.astype(jnp.float16), "rep", 0, 0)), axis=0)


def solution(mesh):
    return jax.shard_map(
        local,
        mesh=mesh,
        in_specs=(P("row", "col"), P("row", "col"), P("row", "col")),
        out_specs=P(("row", "rep"), "col"),
        check_vma=False,
    )
```

```python
import functools

import jax
import jax.numpy as jnp
from jax import lax
from jax.experimental import pallas as pl
from jax.experimental.pallas import tpu as pltpu
from jax.sharding import PartitionSpec as P

BLK = 128
TOP = 8192.0
LOWEST, HIGHEST = -100.0, 126.0
HEAD = 8

SMEM = pl.BlockSpec(memory_space=pltpu.SMEM)
VMEM = pl.BlockSpec(memory_space=pltpu.VMEM)
HBM = pl.BlockSpec(memory_space=pltpu.HBM)


def call(kernel, out_shape, in_specs, scratch=()):
    return pl.pallas_call(
        kernel,
        out_shape=out_shape,
        in_specs=in_specs,
        scratch_shapes=list(scratch),
        compiler_params=pltpu.CompilerParams(vmem_limit_bytes=32 << 20),
    )


def contract(a, b):
    return lax.dot_general(a, b, (((0,), (0,)), ((), ())), preferred_element_type=jnp.float32)


def scaled(values):
    largest = jnp.max(jnp.abs(values), axis=0, keepdims=True)
    exponent = jnp.floor(jnp.log2(jnp.maximum(largest, 2.0**LOWEST)))
    exponent = jnp.clip(exponent, LOWEST, HIGHEST)
    return values * jnp.exp2(-exponent) * TOP, exponent


def store_coded(ref, values):
    coded, exponent = scaled(values)
    height = values.shape[0]
    ref[:height, :] = coded.astype(ref.dtype)
    ref[height:, :] = jnp.broadcast_to(exponent, (HEAD, values.shape[1])).astype(ref.dtype)


def store_packed(ref, values):
    coded, exponent = scaled(values)
    height, width = values.shape
    groups = width // BLK
    for group in range(groups):
        columns = slice(group * BLK, (group + 1) * BLK)
        ref[group * height : (group + 1) * height, :] = coded[:, columns].astype(ref.dtype)
    rows = [exponent[:, group * BLK : (group + 1) * BLK] for group in range(groups)]
    rows.append(jnp.zeros((HEAD - groups, BLK), jnp.float32))
    ref[groups * height :, :] = jnp.concatenate(rows, axis=0).astype(ref.dtype)


def decode(pieces):
    count, height, width = pieces.shape
    height -= HEAD
    scale = jnp.exp2(pieces[:, height:, :].astype(jnp.float32)) * (1.0 / TOP)
    scale = jnp.broadcast_to(scale[:, None], (count, height // HEAD, HEAD, width))
    return pieces[:, :height, :].astype(jnp.float32) * scale.reshape(count, height, width)


def gather(packed, axis, groups):
    whole = lax.all_gather(packed.astype(jnp.float16), axis)
    count, height = whole.shape[0], whole.shape[1] - HEAD
    scale = jnp.exp2(whole[:, height : height + groups, :].astype(jnp.float32)) * (1.0 / TOP)
    scale = jnp.broadcast_to(scale[:, :, None, :], (count, groups, height // groups, BLK))
    values = whole[:, :height, :].astype(jnp.float32) * scale.reshape(count, height, BLK)
    return values.astype(jnp.bfloat16)


def panel(ref, groups):
    count, height, _ = ref.shape
    height //= groups
    columns = [
        ref[:, group * height : (group + 1) * height, :].reshape(count * height, BLK)
        for group in range(groups)
    ]
    return jnp.concatenate(columns, axis=1)


def window_start(start, rows, width):
    return pl.multiple_of(jnp.minimum(lax.div(start, BLK) * BLK, rows - width), BLK)


def prepare(own, halves, rep_ref, tile_ref, right_ref, left_ref, tile, turned, arrived):
    rows = tile_ref.shape[0]
    copies = [
        pltpu.make_async_copy(
            tile_ref.at[part * BLK : (part + 1) * BLK, :],
            tile.at[part * BLK : (part + 1) * BLK, :],
            arrived.at[part],
        )
        for part in range(rows // BLK)
    ]
    for copy in copies:
        copy.start()
    start = pl.multiple_of(rep_ref[0] * own, own)
    width = turned.shape[1]
    first = window_start(start, rows, width)
    for part, copy in enumerate(copies):
        copy.wait()
        at = slice(part * BLK, (part + 1) * BLK)
        for half in range(halves):
            columns = pl.ds(pl.multiple_of(half * rows + first, BLK), width)
            turned[half, :, at] = tile[at, columns].T
    for half in range(halves):
        piece = turned[half, pl.ds(pl.multiple_of(start - first, 16), own), :]
        for to in range(left_ref.shape[0]):
            left_ref[to, half * own : (half + 1) * own, :] = piece
    store_packed(right_ref, tile[pl.ds(start, own), :].astype(jnp.float32))


def square_part(own, halves, right_ref, left_ref, out_ref):
    product = contract(left_ref[...], panel(right_ref, right_ref.shape[1] // own)).T
    rows = product.shape[0] // halves
    for rep in range(out_ref.shape[0]):
        for half in range(halves):
            first = half * rows + rep * own
            out_ref[rep, half * own : (half + 1) * own, :] = product[first : first + own, :]


def square_sum(own, halves, rep_ref, keep_ref, later_ref, parts_ref, square_ref, low_ref, factor_ref):
    total = parts_ref[0]
    for rep in range(1, parts_ref.shape[0]):
        total = total + parts_ref[rep]
    rows = parts_ref.shape[2]
    per_half = rows // BLK
    start = rep_ref[0] * own
    for half in range(halves):
        block = lax.div(lax.broadcasted_iota(jnp.int32, (own, BLK), 0) + start, BLK)
        for across in range(rows // BLK):
            kept = jnp.zeros((own, BLK), jnp.float32)
            for down in range(per_half):
                keep = keep_ref[across, half * per_half + down].astype(jnp.float32)
                kept = jnp.where(block == down, keep, kept)
            at = slice(half * own, (half + 1) * own), slice(across * BLK, (across + 1) * BLK)
            square_ref[at] = total[at] * kept
    for down in range(later_ref.shape[0]):
        for across in range(later_ref.shape[1]):
            factor = -2.0 * later_ref[down, across].astype(jnp.float32)
            factor_ref[down, :, across * BLK : (across + 1) * BLK] = jnp.full((8, BLK), factor)
    store_packed(low_ref, square_ref[...].astype(jnp.bfloat16).astype(jnp.float32))


def cube_part(own, halves, rep_ref, factor_ref, low_ref, right_ref, square_ref, out_ref, placed, total):
    rows, cols = total.shape
    start = pl.multiple_of(rep_ref[0] * own, own)
    placed[...] = jnp.zeros_like(placed)
    for half in range(halves):
        placed[pl.ds(pl.multiple_of(half * rows + start, own), own), :] = (
            3.0 * square_ref[half * own : (half + 1) * own, :]
        )
    product = contract(panel(low_ref, rows // BLK), panel(right_ref, cols // BLK))
    for down in range(rows // BLK):
        for across in range(cols // BLK):
            at = slice(down * BLK, (down + 1) * BLK), slice(across * BLK, (across + 1) * BLK)
            total[at] = placed[at[1], at[0]].T + factor_ref[down, :1, at[1]] * product[at]
    for rep in range(out_ref.shape[0]):
        store_coded(out_ref.at[rep], total[rep * own : (rep + 1) * own, :])


def local(density, keep_square, keep_cube):
    rows, cols = density.shape
    reps, col_count = lax.axis_size("rep"), lax.axis_size("col")
    own, halves = rows // reps, cols // rows
    rep = lax.axis_index("rep").astype(jnp.int32).reshape(1)
    shape = jax.ShapeDtypeStruct
    part = halves * own
    width = -(-own // BLK) * BLK + BLK

    right_coded, left_copies = call(
        functools.partial(prepare, own, halves),
        (
            shape((own * (cols // BLK) + HEAD, BLK), jnp.bfloat16),
            shape((col_count, part, rows), jnp.bfloat16),
        ),
        [SMEM, HBM],
        [
            pltpu.VMEM((rows, cols), jnp.bfloat16),
            pltpu.VMEM((halves, width, rows), jnp.bfloat16),
            pltpu.SemaphoreType.DMA((rows // BLK,)),
        ],
    )(rep, pltpu.with_memory_space_constraint(density, pltpu.HBM))
    left = lax.all_to_all(left_copies, "col", 0, 0).reshape(col_count * part, rows)
    right = gather(right_coded, "row", cols // BLK)
    parts = call(
        functools.partial(square_part, own, halves),
        shape((reps, part, rows), jnp.float32),
        [VMEM, VMEM],
    )(right, left)
    parts = lax.all_to_all(parts, "rep", 0, 0)
    square, low_coded, factor = call(
        functools.partial(square_sum, own, halves),
        (
            shape((part, rows), jnp.float32),
            shape((part * (rows // BLK) + HEAD, BLK), jnp.bfloat16),
            shape((rows // BLK, 8, cols), jnp.float32),
        ),
        [SMEM, SMEM, SMEM, VMEM],
    )(rep, keep_square, keep_cube, parts)
    low = gather(low_coded, "col", rows // BLK)
    total = call(
        functools.partial(cube_part, own, halves),
        shape((reps, own + HEAD, cols), jnp.float32),
        [SMEM, VMEM, VMEM, VMEM, VMEM],
        [pltpu.VMEM((cols, rows), jnp.float32), pltpu.VMEM((rows, cols), jnp.float32)],
    )(rep, factor, low, right, square)
    return jnp.sum(decode(lax.all_to_all(total.astype(jnp.float16), "rep", 0, 0)), axis=0)


def solution(mesh):
    return jax.shard_map(
        local,
        mesh=mesh,
        in_specs=(P("row", "col"), P("row", "col"), P("row", "col")),
        out_specs=P(("row", "rep"), "col"),
        check_vma=False,
    )
```
